512 devices in a mesh: tm: 64 (over y_hi, x, z), rows: 8 (over y_lo, core).
Axes of the slice: x: 4, y: 8 (y_hi: 2, y_lo: 4; y = y_hi * 4 + y_lo), z: 8, core: 2. Of those that a mesh axis runs over, the one named last changes fastest.
Arguments:
- frames: bfloat16 [128, 16, 160, 256], P('tm', 'rows'), may hold values from -500 to 500
- norm_gain: float32 [256], replicated, may hold values from 0.1 to 1.9
- norm_shift: float32 [256], replicated, may hold values from -3 to 3
- conv_weight: bfloat16 [3, 3, 3, 256, 256], replicated, may hold values from -0.078125 to 0.078125
- conv_bias: float32 [256], replicated, may hold values from -3 to 3
Outputs:
- decoded: bfloat16 [128, 16, 160, 256], P('tm', 'rows')
The draws below stay inside these ranges and needn't reach their ends.
All inputs are finite; a program needn't handle non-finite values.
Results may differ from the reference program's by a relative error of at most 0.0043.
Values may be sent and summed in bfloat16 or wider, within the bound.
A program may use at most 64 MiB of HBM per device.

```python
import math
import jax
import jax.numpy as jnp
from jax import lax

CHANNELS = 256
GROUPS = 32
WIDTH = 160
FRAMES = 128
HEIGHT = 16


def draw_frames(key, part):
    key = jax.random.fold_in(key, 11)
    keys = jax.random.split(key, 3)
    shape_full = (FRAMES, HEIGHT, WIDTH, CHANNELS)
    noise = jnp.clip(jax.random.normal(keys[0], shape_full, jnp.float32), -4.0, 4.0)
    ramp = jnp.arange(FRAMES, dtype=jnp.float32) / max(FRAMES - 1, 1)
    trend = jnp.exp(ramp * math.log(3.0)).reshape(-1, 1, 1, 1)
    row_scale = jnp.exp(jax.random.uniform(keys[1], (FRAMES, HEIGHT, 1, 1), jnp.float32) * math.log(10.0))
    channel_scale = jnp.exp(jax.random.uniform(keys[2], (1, 1, 1, CHANNELS), jnp.float32) * math.log(10.0))
    return (noise * trend * row_scale * channel_scale / 3.0).astype(jnp.bfloat16)


def gaussian(own_key, dims, scale, reach, kind=jnp.bfloat16):
    return jnp.clip(scale * jax.random.normal(own_key, dims, jnp.float32), -reach, reach).astype(kind)


def setup_inputs(seed: int = 0) -> dict:
    streams_of = jax.random.split(jax.random.key(seed), 6)
    frames = draw_frames(jax.random.fold_in(streams_of[5], 71), 0)
    norm_gain = jnp.clip(1.0 + 0.18 * jax.random.normal(streams_of[1], (CHANNELS,), jnp.float32), 0.1, 1.9)
    norm_shift = gaussian(streams_of[2], (CHANNELS,), 0.5, 3.0, jnp.float32)
    conv_weight = gaussian(streams_of[3], (3, 3, 3, CHANNELS, CHANNELS), (27 * CHANNELS) ** -0.5, 0.078125)
    conv_bias = gaussian(streams_of[4], (CHANNELS,), 0.5, 3.0, jnp.float32)
    return dict(frames=frames, norm_gain=norm_gain, norm_shift=norm_shift, conv_weight=conv_weight, conv_bias=conv_bias)


def reference(frames, norm_gain, norm_shift, conv_weight, conv_bias):
    channels = frames.shape[-1]
    group_width = channels // GROUPS
    cell_count = FRAMES * HEIGHT * WIDTH * group_width

    def frame_sum(single):
        return lax.optimization_barrier(jnp.sum(single.astype(jnp.float32).reshape(-1, GROUPS, group_width), axis=(0, 2)))
    group_mean = lax.optimization_barrier(jnp.sum(lax.map(frame_sum, frames), axis=0)) / cell_count
    mean_c = jnp.repeat(group_mean, group_width)

    def frame_square(single):
        centred = single.astype(jnp.float32) - mean_c
        return lax.optimization_barrier(jnp.sum((centred * centred).reshape(-1, GROUPS, group_width), axis=(0, 2)))
    group_var = lax.optimization_barrier(jnp.sum(lax.map(frame_square, frames), axis=0)) / cell_count
    scale_c = jnp.repeat(lax.rsqrt(group_var + 1e-06), group_width)

    def activate(single):
        normed = (single.astype(jnp.float32) - mean_c) * scale_c * norm_gain + norm_shift
        return jax.nn.silu(normed).astype(jnp.bfloat16)
    activated = lax.map(activate, frames)
    padded = jnp.pad(activated, ((2, 0), (1, 1), (1, 1), (0, 0)), mode='edge')

    def out_frame(start):
        window = lax.dynamic_slice_in_dim(padded, start.astype(jnp.int32), 3, 0)
        running = jnp.zeros((HEIGHT * WIDTH, channels), jnp.float32)
        for step_t in range(3):
            for step_y in range(3):
                strip = window[step_t, step_y:step_y + HEIGHT]
                columns = jnp.concatenate([strip[:, step_x:step_x + WIDTH] for step_x in range(3)], axis=-1)
                kernel = conv_weight[step_t, step_y].reshape(3 * channels, channels)
                running = running + jnp.dot(columns.reshape(HEIGHT * WIDTH, 3 * channels), kernel, preferred_element_type=jnp.float32)
        return (running + conv_bias).astype(jnp.bfloat16).reshape(HEIGHT, WIDTH, channels)
    return lax.map(out_frame, jnp.arange(FRAMES, dtype=jnp.int32))
```

```python
import functools

import jax
import jax.numpy as jnp
from jax import lax
from jax.experimental import pallas as pl
from jax.experimental.pallas import tpu as pltpu
from jax.sharding import PartitionSpec as P

GROUPS = 32
MESH = pl.DeviceIdType.MESH
NX, NZ, NYLO, NCORE = 4, 8, 4, 2
NY = 8
TM, ROWS = 64, 8
STAGE_SIZES = (NX * NCORE, NZ, NY)


def position():
    t, r = lax.axis_index("tm"), lax.axis_index("rows")
    return (t // NZ) % NX, (t // (NX * NZ)) * NYLO + r // NCORE, t % NZ, r % NCORE


def device(x, y, z, core):
    return {"tm": (y // NYLO) * (NX * NZ) + x * NZ + z, "rows": (y % NYLO) * NCORE + core}


def stage_slot(stage):
    x, y, z, core = position()
    return (x * NCORE + core, z, y)[stage]


def stage_peer(stage, k):
    x, y, z, core = position()
    if stage == 0:
        other = (x * NCORE + core + k) % STAGE_SIZES[0]
        return device(other // NCORE, y, z, other % NCORE)
    if stage == 1:
        return device(x, y, (z + k) % NZ, core)
    return device(x, (y + k) % NY, z, core)


def remote(src, dst, send, recv, where):
    return pltpu.make_async_remote_copy(
        src_ref=src, dst_ref=dst, send_sem=send, recv_sem=recv, device_id=where, device_id_type=MESH
    )


def group_fold(v, group_width):
    lanes = v.shape[-1]
    lane = lax.broadcasted_iota(jnp.int32, v.shape, v.ndim - 1)
    step = 1
    while step < group_width:
        ahead = pltpu.roll(v, lanes - step, v.ndim - 1)
        behind = pltpu.roll(v, step, v.ndim - 1)
        v = v + jnp.where((lane // step) % 2 == 0, ahead, behind)
        step *= 2
    return v


def kernel(
    frames, gain, shift, weight, bias, out,
    raw, act, taps, acc, stats,
    own_sem, taps_sem, prev_send, prev_recv, row_send, row_recv, fwd_send, fwd_recv, stat_send, stat_recv,
):
    frame_count, row_count, width, channels = frames.shape
    group_width = channels // GROUPS
    cells = frame_count * row_count * width
    t, r = lax.axis_index("tm"), lax.axis_index("rows")
    has_prev, has_next = t > 0, t < TM - 1
    has_above, has_below = r > 0, r < ROWS - 1
    next_dev, prev_dev = {"tm": t + 1, "rows": r}, {"tm": t - 1, "rows": r}
    above_dev, below_dev = {"tm": t, "rows": r - 1}, {"tm": t, "rows": r + 1}

    barrier = pltpu.get_barrier_semaphore()
    peers = 0
    for stage, size in enumerate(STAGE_SIZES):
        for k in range(1, size):
            pl.semaphore_signal(barrier, inc=1, device_id=stage_peer(stage, k), device_id_type=MESH)
            peers += 1
    for there, where in ((has_prev, prev_dev), (has_above, above_dev), (has_below, below_dev)):

        @pl.when(there)
        def _():
            pl.semaphore_signal(barrier, inc=1, device_id=where, device_id_type=MESH)

    own_copy = pltpu.make_async_copy(frames, raw.at[2:4, 1:3], own_sem)
    own_copy.start()
    taps_copy = pltpu.make_async_copy(weight, taps, taps_sem)
    taps_copy.start()
    own_copy.wait()

    mine = raw[2:4, 1:3].reshape(cells, channels).astype(jnp.float32)
    count = float(cells * group_width)
    local_sum = jnp.sum(mine, axis=0, keepdims=True)
    local_mean = group_fold(local_sum, group_width) / count
    centred = mine - local_mean
    local_square = group_fold(jnp.sum(centred * centred, axis=0, keepdims=True), group_width)

    pl.semaphore_wait(
        barrier,
        peers + has_next.astype(jnp.int32) + has_above.astype(jnp.int32) + has_below.astype(jnp.int32),
    )

    def stage_start(stage, mean, square):
        slot = stage_slot(stage)
        stats[stage, slot] = jnp.concatenate([mean, square], axis=0)
        piece = stats.at[stage, slot]
        for k in range(1, STAGE_SIZES[stage]):
            remote(piece, piece, stat_send.at[stage], stat_recv.at[stage], stage_peer(stage, k)).start()

    def stage_finish(stage, n):
        size = STAGE_SIZES[stage]
        rest = stats.at[stage, pl.ds(0, size - 1)]
        pltpu.make_async_copy(rest, rest, stat_recv.at[stage]).wait()
        means, squares = stats[stage, :, 0:1, :], stats[stage, :, 1:2, :]
        mean = jnp.sum(means, axis=0) / size
        apart = means - mean[None]
        return mean, jnp.sum(squares, axis=0) + n * jnp.sum(apart * apart, axis=0), n * size

    stage_start(0, local_mean, local_square)

    prev_copies = [
        [
            remote(frames.at[f, y], raw.at[f, 1 + y], prev_send.at[f, y], prev_recv.at[f, y], next_dev)
            for y in range(2)
        ]
        for f in range(2)
    ]
    to_below = remote(frames.at[:, 1], raw.at[2:4, 0], row_send.at[0], row_recv.at[0], below_dev)
    to_above = remote(frames.at[:, 0], raw.at[2:4, 3], row_send.at[1], row_recv.at[1], above_dev)

    @pl.when(has_next)
    def _():
        for f in range(2):
            for y in range(2):
                prev_copies[f][y].start()

    @pl.when(has_below)
    def _():
        to_below.start()

    @pl.when(has_above)
    def _():
        to_above.start()

    mean, square, n = stage_finish(0, count)
    stage_start(1, mean, square)
    mean, square, n = stage_finish(1, n)
    stage_start(2, mean, square)

    pass_below = remote(raw.at[0:2, 2], raw.at[0:2, 0], fwd_send.at[0], fwd_recv.at[0], below_dev)
    pass_above = remote(raw.at[0:2, 1], raw.at[0:2, 3], fwd_send.at[1], fwd_recv.at[1], above_dev)

    def forward():
        for y, there, copy in ((0, has_above, pass_above), (1, has_below, pass_below)):
            for f in range(2):
                prev_copies[f][y].wait_recv()

            @pl.when(there)
            def _():
                copy.start()

    far = t == TM // 2

    @pl.when(has_prev & jnp.logical_not(far))
    def _():
        forward()

    mean, square, n = stage_finish(2, n)
    scale = lax.rsqrt(square / n + 1e-06) * gain[...]
    half_scale, half_shift = 0.5 * scale, 0.5 * shift[...]

    def activate(f, y, src_f, src_y):
        h = (raw[src_f, src_y].astype(jnp.float32) - mean) * half_scale + half_shift
        act[f, y] = (h + h * jnp.tanh(h)).astype(jnp.bfloat16)

    top = jnp.where(has_above, 0, 1)
    bottom = jnp.where(has_below, 3, 2)

    def window(a, frame_ids):
        parts = [act[frame_ids, b : b + 2] for b in range(3)]
        return jnp.concatenate([p.reshape(-1, channels) for p in parts], axis=-1)

    def tap(a, c):
        return jnp.concatenate([taps[a, b, c] for b in range(3)], axis=0)

    def dot(lhs, rhs):
        return jnp.dot(lhs, rhs, preferred_element_type=jnp.float32)

    for f in (2, 3):
        for y in (1, 2):
            activate(f, y, f, y)

    @pl.when(has_above)
    def _():
        to_below.wait_recv()

    @pl.when(has_below)
    def _():
        to_above.wait_recv()

    for f in (2, 3):
        activate(f, 0, f, top)
        activate(f, 3, f, bottom)
    taps_copy.wait()

    half = row_count * width
    both, late = window(2, slice(2, 4)), window(1, slice(2, 3))
    for c in range(3):
        acc[c] = dot(both, tap(2, c))
        acc[c, half:] += dot(late, tap(1, c))

    @pl.when(has_prev & far)
    def _():
        forward()

    src = [jnp.where(has_prev, f, 2) for f in range(2)]
    for f in range(2):
        for y in (1, 2):
            activate(f, y, src[f], y)

    @pl.when(has_prev & has_above)
    def _():
        pass_below.wait_recv()

    @pl.when(has_prev & has_below)
    def _():
        pass_above.wait_recv()

    for f in range(2):
        activate(f, 0, src[f], top)
        activate(f, 3, src[f], bottom)

    both, early = window(0, slice(0, 2)), window(1, slice(1, 2))
    for c in range(3):
        acc[c] += dot(both, tap(0, c))
        acc[c, :half] += dot(early, tap(1, c))

    column = lax.broadcasted_iota(jnp.int32, (width, channels), 0)
    for f in range(2):
        for y in range(2):
            rows = pl.ds((f * row_count + y) * width, width)
            left, right = acc[0, rows], acc[2, rows]
            left = jnp.where(column == 0, left, pltpu.roll(left, 1, 0))
            right = jnp.where(column == width - 1, right, pltpu.roll(right, width - 1, 0))
            out[f, y] = (left + acc[1, rows] + right + bias[...]).astype(jnp.bfloat16)

    @pl.when(has_next)
    def _():
        for f in range(2):
            for y in range(2):
                prev_copies[f][y].wait_send()

    @pl.when(has_below)
    def _():
        to_below.wait_send()

    @pl.when(has_above)
    def _():
        to_above.wait_send()

    @pl.when(has_prev & has_below)
    def _():
        pass_below.wait_send()

    @pl.when(has_prev & has_above)
    def _():
        pass_above.wait_send()

    for stage, size in enumerate(STAGE_SIZES):
        rest = stats.at[stage, pl.ds(0, size - 1)]
        pltpu.make_async_copy(rest, rest, stat_send.at[stage]).wait()


def local(frames, norm_gain, norm_shift, conv_weight, conv_bias):
    frame_count, row_count, width, channels = frames.shape
    vmem, anywhere = pl.BlockSpec(memory_space=pltpu.VMEM), pl.BlockSpec(memory_space=pl.ANY)
    dma = pltpu.SemaphoreType.DMA
    cells = frame_count * row_count * width
    return pl.pallas_call(
        kernel,
        out_shape=jax.ShapeDtypeStruct(frames.shape, jnp.bfloat16),
        in_specs=[anywhere, vmem, vmem, anywhere, vmem],
        out_specs=vmem,
        scratch_shapes=[
            pltpu.VMEM((4, 4, width, channels), jnp.bfloat16),
            pltpu.VMEM((4, 4, width, channels), jnp.bfloat16),
            pltpu.VMEM(conv_weight.shape, jnp.bfloat16),
            pltpu.VMEM((3, cells, channels), jnp.float32),
            pltpu.VMEM((3, 8, 2, channels), jnp.float32),
            dma, dma, dma((2, 2)), dma((2, 2)), dma((2,)), dma((2,)), dma((2,)), dma((2,)), dma((3,)), dma((3,)),
        ],
        compiler_params=pltpu.CompilerParams(
            collective_id=0, has_side_effects=True, vmem_limit_bytes=40 * 1024 * 1024
        ),
        name="norm_conv",
    )(
        frames,
        norm_gain.reshape(1, channels),
        norm_shift.reshape(1, channels),
        conv_weight,
        conv_bias.reshape(1, channels),
    )


def solution(mesh):
    in_specs = (P("tm", "rows", None, None), P(), P(), P(), P())
    out_specs = P("tm", "rows", None, None)
    return jax.shard_map(local, mesh=mesh, in_specs=in_specs, out_specs=out_specs, check_vma=False)
```

```python
import itertools
import math

import jax
import jax.numpy as jnp
from jax import lax
from jax.experimental import pallas as pl
from jax.experimental.pallas import tpu as pltpu
from jax.sharding import PartitionSpec as P

GROUPS = 32
MESH = pl.DeviceIdType.MESH
TM, ROWS = 64, 8
SIZE = {"x": 4, "y": 8, "z": 8, "core": 2}
STAGES = (("z", "core"), ("x", "y"))
SLOTS = max(math.prod(SIZE[a] for a in axes) for axes in STAGES)
FAR = TM // 2
RELAYS = (7, 24)


def coordinates(t, r):
    return {"x": (t >> 3) & 3, "y": ((t >> 5) << 2) + (r >> 1), "z": t & 7, "core": r & 1}


def device(at):
    y = at["y"]
    return {"tm": ((y >> 2) << 5) + (at["x"] << 3) + at["z"], "rows": ((y & 3) << 1) + at["core"]}


def stage_size(stage):
    return math.prod(SIZE[a] for a in STAGES[stage])


def stage_slot(stage, at):
    slot = 0
    for axis in STAGES[stage]:
        slot = slot * SIZE[axis] + at[axis]
    return slot


def stage_peers(stage, at):
    axes = STAGES[stage]
    steps = list(itertools.product(*(range(SIZE[a]) for a in axes)))[1:]
    hops = lambda step: sum(min(k, SIZE[a] - k) for a, k in zip(axes, step) if a != "core")
    steps.sort(key=hops, reverse=True)
    return [device(at | {a: (at[a] + k) & (SIZE[a] - 1) for a, k in zip(axes, step)}) for step in steps]


def remote(src, dst, send, recv, where):
    return pltpu.make_async_remote_copy(
        src_ref=src, dst_ref=dst, send_sem=send, recv_sem=recv, device_id=where, device_id_type=MESH
    )


def group_fold(v, group_width):
    lanes = v.shape[-1]
    lane = lax.broadcasted_iota(jnp.int32, v.shape, v.ndim - 1)
    step = 1
    while step < group_width:
        ahead = pltpu.roll(v, lanes - step, v.ndim - 1)
        behind = pltpu.roll(v, step, v.ndim - 1)
        v = v + jnp.where((lane // step) % 2 == 0, ahead, behind)
        step *= 2
    return v


def kernel(
    frames, gain_hbm, shift_hbm, weight, bias_hbm, out,
    raw, act, taps, acc, relayed, stats, gain, shift, bias,
    relay_send, relay_recv, vec_sem, own_sem, taps_sem, prev_send, prev_recv, row_send, row_recv, fwd_send, fwd_recv, stat_send, stat_recv,
):
    frame_count, row_count, width, channels = frames.shape
    group_width = channels // GROUPS
    cells = frame_count * row_count * width
    t, r = lax.axis_index("tm"), lax.axis_index("rows")
    has_prev, has_next = t > 0, t < TM - 1
    has_above, has_below = r > 0, r < ROWS - 1
    next_dev, prev_dev = {"tm": t + 1, "rows": r}, {"tm": t - 1, "rows": r}
    above_dev, below_dev = {"tm": t, "rows": r - 1}, {"tm": t, "rows": r + 1}

    at = coordinates(t, r)
    peers = [stage_peers(stage, at) for stage in range(len(STAGES))]
    far_sender, far = t == FAR - 1, t == FAR
    is_relay = [t == place for place in RELAYS]
    relay_devs = [{"tm": place, "rows": r} for place in RELAYS]
    far_dev = {"tm": FAR, "rows": r}

    barrier = pltpu.get_barrier_semaphore()
    for where in sum(peers, []):
        pl.semaphore_signal(barrier, inc=1, device_id=where, device_id_type=MESH)
    greeted = [(has_prev, prev_dev), (has_above, above_dev), (has_below, below_dev)]
    for there, where in greeted + [(far, where) for where in relay_devs]:

        @pl.when(there)
        def _():
            pl.semaphore_signal(barrier, inc=1, device_id=where, device_id_type=MESH)

    own_copy = pltpu.make_async_copy(frames, raw.at[2:4, 1:3], own_sem)
    own_copy.start()
    taps_copy = pltpu.make_async_copy(weight, taps, taps_sem)
    taps_copy.start()
    vec_copies = [
        pltpu.make_async_copy(src, dst, vec_sem.at[i])
        for i, (src, dst) in enumerate(((gain_hbm, gain), (shift_hbm, shift), (bias_hbm, bias)))
    ]
    for copy in vec_copies:
        copy.start()
    own_copy.wait()

    mine = raw[2:4, 1:3].reshape(cells, channels).astype(jnp.float32)
    count = float(cells * group_width)
    local_sum = jnp.sum(mine, axis=0, keepdims=True)
    local_mean = group_fold(local_sum, group_width) / count
    centred = mine - local_mean
    local_square = group_fold(jnp.sum(centred * centred, axis=0, keepdims=True), group_width)

    pl.semaphore_wait(
        barrier,
        len(sum(peers, []))
        + sum(there.astype(jnp.int32) for there in [has_next, has_above, has_below, *is_relay]),
    )

    def stage_start(stage, mean, square):
        slot = stage_slot(stage, at)
        stats[stage, slot] = jnp.concatenate([mean, square], axis=0)
        piece = stats.at[stage, slot]
        for where in peers[stage]:
            remote(piece, piece, stat_send.at[stage], stat_recv.at[stage], where).start()

    def stage_finish(stage, n):
        size = stage_size(stage)
        rest = stats.at[stage, pl.ds(0, size - 1)]
        pltpu.make_async_copy(rest, rest, stat_recv.at[stage]).wait()
        means, squares = stats[stage, 0:size, 0:1, :], stats[stage, 0:size, 1:2, :]
        mean = jnp.sum(means, axis=0) / size
        apart = means - mean[None]
        return mean, jnp.sum(squares, axis=0) + n * jnp.sum(apart * apart, axis=0), n * size

    stage_start(0, local_mean, local_square)

    prev_copies = [
        [
            remote(frames.at[f, y], raw.at[f, 1 + y], prev_send.at[f, y], prev_recv.at[f, y], next_dev)
            for y in range(2)
        ]
        for f in range(2)
    ]
    to_below = remote(frames.at[:, 1], raw.at[2:4, 0], row_send.at[0], row_recv.at[0], below_dev)
    to_above = remote(frames.at[:, 0], raw.at[2:4, 3], row_send.at[1], row_recv.at[1], above_dev)

    @pl.when(has_next)
    def _():
        for y in range(2):
            prev_copies[0][y].start()

    @pl.when(has_next & jnp.logical_not(far_sender))
    def _():
        for y in range(2):
            prev_copies[1][y].start()

    @pl.when(far_sender)
    def _():
        for y in range(2):
            remote(frames.at[1, y], relayed, prev_send.at[1, y], relay_recv, relay_devs[y]).start()

    @pl.when(has_below)
    def _():
        to_below.start()

    @pl.when(has_above)
    def _():
        to_above.start()

    mean, square, n = stage_finish(0, count)
    stage_start(1, mean, square)

    relay_copies = [remote(relayed, raw.at[1, 1 + y], relay_send, prev_recv.at[1, y], far_dev) for y in range(2)]
    for there, copy, where in zip(is_relay, relay_copies, relay_devs):

        @pl.when(there)
        def _():
            remote(frames.at[1, 0], relayed, relay_send, relay_recv, where).wait_recv()
            copy.start()

    pass_below = remote(raw.at[0:2, 2], raw.at[0:2, 0], fwd_send.at[0], fwd_recv.at[0], below_dev)
    pass_above = remote(raw.at[0:2, 1], raw.at[0:2, 3], fwd_send.at[1], fwd_recv.at[1], above_dev)

    def forward():
        for y, there, copy in ((0, has_above, pass_above), (1, has_below, pass_below)):
            for f in range(2):
                prev_copies[f][y].wait_recv()

            @pl.when(there)
            def _():
                copy.start()

    @pl.when(has_prev & jnp.logical_not(far))
    def _():
        forward()

    for copy in vec_copies:
        copy.wait()
    mean, square, n = stage_finish(1, n)
    scale = lax.rsqrt(square / n + 1e-06) * gain[...]
    half_scale, half_shift = 0.5 * scale, 0.5 * shift[...]

    def activate(f, y, src_f, src_y):
        h = (raw[src_f, src_y].astype(jnp.float32) - mean) * half_scale + half_shift
        act[f, y] = (h + h * jnp.tanh(h)).astype(jnp.bfloat16)

    top = jnp.where(has_above, 0, 1)
    bottom = jnp.where(has_below, 3, 2)

    def window(a, frame_ids):
        parts = [act[frame_ids, b : b + 2] for b in range(3)]
        return jnp.concatenate([p.reshape(-1, channels) for p in parts], axis=-1)

    def tap(a, c):
        return jnp.concatenate([taps[a, b, c] for b in range(3)], axis=0)

    def dot(lhs, rhs):
        return jnp.dot(lhs, rhs, preferred_element_type=jnp.float32)

    for f in (2, 3):
        for y in (1, 2):
            activate(f, y, f, y)

    @pl.when(has_above)
    def _():
        to_below.wait_recv()

    @pl.when(has_below)
    def _():
        to_above.wait_recv()

    for f in (2, 3):
        activate(f, 0, f, top)
        activate(f, 3, f, bottom)
    taps_copy.wait()

    half = row_count * width
    both, late = window(2, slice(2, 4)), window(1, slice(2, 3))
    for c in range(3):
        acc[c] = dot(both, tap(2, c))
        acc[c, half:] += dot(late, tap(1, c))

    @pl.when(has_prev & far)
    def _():
        forward()

    src = [jnp.where(has_prev, f, 2) for f in range(2)]
    for f in range(2):
        for y in (1, 2):
            activate(f, y, src[f], y)

    @pl.when(has_prev & has_above)
    def _():
        pass_below.wait_recv()

    @pl.when(has_prev & has_below)
    def _():
        pass_above.wait_recv()

    for f in range(2):
        activate(f, 0, src[f], top)
        activate(f, 3, src[f], bottom)

    both, early = window(0, slice(0, 2)), window(1, slice(1, 2))
    for c in range(3):
        acc[c] += dot(both, tap(0, c))
        acc[c, :half] += dot(early, tap(1, c))

    column = lax.broadcasted_iota(jnp.int32, (width, channels), 0)
    for f in range(2):
        for y in range(2):
            rows = pl.ds((f * row_count + y) * width, width)
            left, right = acc[0, rows], acc[2, rows]
            left = jnp.where(column == 0, left, pltpu.roll(left, 1, 0))
            right = jnp.where(column == width - 1, right, pltpu.roll(right, width - 1, 0))
            out[f, y] = (left + acc[1, rows] + right + bias[...]).astype(jnp.bfloat16)

    @pl.when(has_next)
    def _():
        for f in range(2):
            for y in range(2):
                prev_copies[f][y].wait_send()

    @pl.when(has_below)
    def _():
        to_below.wait_send()

    @pl.when(has_above)
    def _():
        to_above.wait_send()

    @pl.when(has_prev & has_below)
    def _():
        pass_below.wait_send()

    @pl.when(has_prev & has_above)
    def _():
        pass_above.wait_send()

    for there, copy in zip(is_relay, relay_copies):

        @pl.when(there)
        def _():
            copy.wait_send()

    for stage in range(len(STAGES)):
        rest = stats.at[stage, pl.ds(0, stage_size(stage) - 1)]
        pltpu.make_async_copy(rest, rest, stat_send.at[stage]).wait()


def local(frames, norm_gain, norm_shift, conv_weight, conv_bias):
    frame_count, row_count, width, channels = frames.shape
    hbm = pl.BlockSpec(memory_space=pltpu.HBM)
    dma = pltpu.SemaphoreType.DMA
    cells = frame_count * row_count * width
    return pl.pallas_call(
        kernel,
        out_shape=pltpu.VMEM(frames.shape, jnp.bfloat16),
        in_specs=[hbm] * 5,
        out_specs=pl.BlockSpec(memory_space=pltpu.VMEM),
        scratch_shapes=[
            pltpu.VMEM((4, 4, width, channels), jnp.bfloat16),
            pltpu.VMEM((4, 4, width, channels), jnp.bfloat16),
            pltpu.VMEM(conv_weight.shape, jnp.bfloat16),
            pltpu.VMEM((3, cells, channels), jnp.float32),
            pltpu.VMEM((width, channels), jnp.bfloat16),
            pltpu.VMEM((len(STAGES), SLOTS, 2, channels), jnp.float32),
            pltpu.VMEM((1, channels), jnp.float32),
            pltpu.VMEM((1, channels), jnp.float32),
            pltpu.VMEM((1, channels), jnp.float32),
            dma, dma, dma((3,)), dma, dma, dma((2, 2)), dma((2, 2)), dma((2,)), dma((2,)), dma((2,)), dma((2,)), dma((len(STAGES),)), dma((len(STAGES),)),
        ],
        compiler_params=pltpu.CompilerParams(
            collective_id=0, has_side_effects=True, vmem_limit_bytes=40 * 1024 * 1024
        ),
        name="norm_conv",
    )(
        *(
            pltpu.with_memory_space_constraint(x, pltpu.HBM)
            for x in (
                frames,
                norm_gain.reshape(1, channels),
                norm_shift.reshape(1, channels),
                conv_weight,
                conv_bias.reshape(1, channels),
            )
        )
    )


def solution(mesh):
    in_specs = (P("tm", "rows", None, None), P(), P(), P(), P())
    out_specs = P("tm", "rows", None, None)
    return jax.shard_map(local, mesh=mesh, in_specs=in_specs, out_specs=out_specs, check_vma=False)
```

```python
import jax
import jax.numpy as jnp
from jax import lax
from jax.experimental import pallas as pl
from jax.experimental.pallas import tpu as pltpu
from jax.sharding import PartitionSpec as P

GROUPS = 32
MESH = pl.DeviceIdType.MESH
TM, ROWS = 64, 8
SIZE = {"x": 4, "y": 8, "z": 8, "core": 2}
HUBS = (0, 1, 2)
MEMBERS = {0: (5, 6, 7), 2: (4, 3)}
LINE = SIZE["z"] * SIZE["core"]
PLANE = SIZE["x"] * SIZE["y"]
FAR = TM // 2
PIECES = ((0, 0), (0, 1), (1, 0), (1, 1))
RELAYS = {(0, 1): 7, (1, 0): 30, (1, 1): 23}


def coordinates(t, r):
    return {"x": (t >> 3) & 3, "y": ((t >> 5) << 2) + (r >> 1), "z": t & 7, "core": r & 1}


def device(at):
    y = at["y"]
    return {"tm": ((y >> 2) << 5) + (at["x"] << 3) + at["z"], "rows": ((y & 3) << 1) + at["core"]}


def plane_peers(at):
    nx, ny = SIZE["x"], SIZE["y"]
    steps = [(i, j) for i in range(nx) for j in range(ny)][1:]
    steps.sort(key=lambda step: min(step[0], nx - step[0]) + min(step[1], ny - step[1]), reverse=True)
    return [device(at | {"x": (at["x"] + i) & (nx - 1), "y": (at["y"] + j) & (ny - 1)}) for i, j in steps]


def signal(semaphore, where):
    pl.semaphore_signal(semaphore, inc=1, device_id=where, device_id_type=MESH)


def pack(mean, square):
    half = mean.shape[-1] // 2
    lane = lax.broadcasted_iota(jnp.int32, (1, half), 1) % 4
    upper = jnp.where(lane == 1, mean[:, half:], square[:, half:])
    lower = jnp.where(lane == 0, mean[:, :half], square[:, :half])
    return jnp.where(lane % 2 == 0, lower, upper)


def unpack(packed):
    lane = lax.broadcasted_iota(jnp.int32, packed.shape, 1) % 4
    rows = jnp.concatenate([jnp.where(lane == k, packed, 0.0) for k in range(4)], axis=0)
    rows = group_fold(rows, 4)
    return jnp.concatenate([rows[0:1], rows[1:2]], axis=1), jnp.concatenate([rows[2:3], rows[3:4]], axis=1)


def combine(parts, n):
    added = jnp.sum(parts, axis=0)
    mean = added / parts.shape[0]
    apart = parts - mean[None]
    spread = pltpu.roll(jnp.sum(apart * apart, axis=0), 2, 1)
    lane = lax.broadcasted_iota(jnp.int32, mean.shape, 1) % 4
    return jnp.where(lane < 2, mean, added + n * spread)


def remote(src, dst, send, recv, where):
    return pltpu.make_async_remote_copy(
        src_ref=src, dst_ref=dst, send_sem=send, recv_sem=recv, device_id=where, device_id_type=MESH
    )


def group_fold(v, group_width):
    lanes = v.shape[-1]
    lane = lax.broadcasted_iota(jnp.int32, v.shape, v.ndim - 1)
    step = 1
    while step < group_width:
        ahead = pltpu.roll(v, lanes - step, v.ndim - 1)
        behind = pltpu.roll(v, step, v.ndim - 1)
        v = v + jnp.where((lane // step) % 2 == 0, ahead, behind)
        step *= 2
    return v


def kernel(
    frames, gain_hbm, shift_hbm, weight, bias_hbm, out,
    raw, act, taps, acc, relayed, line, plane, total, gain, shift, bias,
    vec_sem, own_sem, taps_sem, line_send, line_recv, plane_send, plane_recv, total_send, total_recv, pair_send, prev_send, prev_recv, row_send, row_recv,
    fwd_send, fwd_recv, relay_send, relay_recv,
):
    frame_count, row_count, width, channels = frames.shape
    group_width = channels // GROUPS
    cells = frame_count * row_count * width
    t, r = lax.axis_index("tm"), lax.axis_index("rows")
    has_prev, has_next = t > 0, t < TM - 1
    core = r & 1
    outer, inner = core, 1 - core
    has_cross = (r > 0) & (r < ROWS - 1)
    next_dev, prev_dev = {"tm": t + 1, "rows": r}, {"tm": t - 1, "rows": r}
    cross_dev, partner_dev = {"tm": t, "rows": r + 2 * core - 1}, {"tm": t, "rows": r + 1 - 2 * core}
    outer_slot, inner_slot = 3 - 3 * core, 3 * core

    at = coordinates(t, r)
    is_hub = (at["z"] <= HUBS[-1]) & (core == 1)
    hubs = [(at["z"] == z) & (core == 1) for z in HUBS]
    hub_devs = [device(at | {"z": z, "core": 1}) for z in HUBS]
    peers = plane_peers(at)
    line_slot, plane_slot = 2 * at["z"] + core, SIZE["y"] * at["x"] + at["y"]
    far_sender, far = t == FAR - 1, t == FAR
    is_relay = {piece: t == place for piece, place in RELAYS.items()}
    relay_devs = {piece: {"tm": place, "rows": r} for piece, place in RELAYS.items()}
    far_dev = {"tm": FAR, "rows": r}

    own_copy = pltpu.make_async_copy(frames, raw.at[2:4, 1:3], own_sem)
    own_copy.start()

    barrier = pltpu.get_barrier_semaphore()

    @pl.when(is_hub)
    def _():
        for dz in (4, 3, 5, 2, 6, 1, 7, 0):
            for dk in range(0 if dz else 1, 2):
                signal(barrier, device(at | {"z": (at["z"] + dz) & 7, "core": (core + dk) & 1}))
        for where in peers:
            signal(barrier, where)

    for hub_z, others in MEMBERS.items():

        @pl.when((at["z"] >= min(others)) & (at["z"] <= max(others)))
        def _():
            signal(barrier, device(at | {"z": hub_z, "core": 1}))

    signal(barrier, partner_dev)
    greeted = [(has_prev, prev_dev), (has_cross, cross_dev)]
    greeted += [(far, where) for where in relay_devs.values()]
    greeted += [(there, {"tm": FAR - 1, "rows": r}) for there in is_relay.values()]
    for there, where in greeted:

        @pl.when(there)
        def _():
            signal(barrier, where)

    vec_copies = [
        pltpu.make_async_copy(src, dst, vec_sem.at[i])
        for i, (src, dst) in enumerate(((gain_hbm, gain), (shift_hbm, shift), (bias_hbm, bias)))
    ]
    for copy in vec_copies:
        copy.start()
    own_copy.wait()
    taps_copy = pltpu.make_async_copy(weight, taps, taps_sem)
    taps_copy.start()

    mine = raw[2:4, 1:3].reshape(cells, channels).astype(jnp.float32)
    count = float(cells * group_width)
    local_sum = jnp.sum(mine, axis=0, keepdims=True)
    local_mean = group_fold(local_sum, group_width) / count
    centred = mine - local_mean
    local_square = group_fold(jnp.sum(centred * centred, axis=0, keepdims=True), group_width)

    greetings = 1 + jnp.where(is_hub, len(peers) - 1, 0) + len(hubs) + len(RELAYS) * far_sender.astype(jnp.int32)
    for hub_z, others in MEMBERS.items():
        greetings += jnp.where((at["z"] == hub_z) & (core == 1), 2 * len(others), 0)
    for there in [has_next, has_cross, *is_relay.values()]:
        greetings += there.astype(jnp.int32)
    pl.semaphore_wait(barrier, greetings)

    mine_ref = line.at[line_slot]
    mine_ref[...] = pack(local_mean, local_square)
    to_hubs = [
        (jnp.logical_not(here), remote(mine_ref, mine_ref, line_send.at[k], line_recv, where))
        for k, (here, where) in enumerate(zip(hubs, hub_devs))
    ]
    for there, copy in to_hubs:

        @pl.when(there)
        def _():
            copy.start()

    prev, onward, relay_in, relay_out = {}, {}, {}, {}
    for kind, f in PIECES:
        y, slot, where = ((outer, outer_slot, cross_dev), (inner, inner_slot, partner_dev))[kind]
        src, dst = frames.at[f, y], raw.at[f, 1 + y]
        prev[kind, f] = remote(src, dst, prev_send.at[kind, f], prev_recv.at[kind, f], next_dev)
        onward[kind, f] = remote(dst, raw.at[f, slot], fwd_send.at[kind, f], fwd_recv.at[kind, f], where)
        if (kind, f) in RELAYS:
            relay_in[kind, f] = remote(src, relayed, prev_send.at[kind, f], relay_recv, relay_devs[kind, f])
            relay_out[kind, f] = remote(relayed, dst, relay_send, prev_recv.at[kind, f], far_dev)
    to_cross = remote(frames.at[:, outer], raw.at[2:4, outer_slot], row_send.at[0], row_recv.at[0], cross_dev)
    to_partner = remote(frames.at[:, inner], raw.at[2:4, inner_slot], row_send.at[1], row_recv.at[1], partner_dev)

    @pl.when(has_next)
    def _():
        prev[0, 0].start()

    @pl.when(has_next & jnp.logical_not(far_sender))
    def _():
        prev[0, 1].start()

    @pl.when(far_sender)
    def _():
        for copy in relay_in.values():
            copy.start()

    @pl.when(has_cross)
    def _():
        to_cross.start()

    to_partner.start()

    @pl.when(has_next & jnp.logical_not(far_sender))
    def _():
        for f in range(2):
            prev[0, f].wait_send()
        for f in range(2):
            prev[1, f].start()

    for piece, there in is_relay.items():

        @pl.when(there)
        def _():
            relay_in[piece].wait_recv()
            relay_out[piece].start()

    plane_ref = plane.at[plane_slot]
    to_peers = [remote(plane_ref, plane_ref, plane_send, plane_recv, where) for where in peers]
    to_members = {
        hub_z: [
            remote(total, total, total_send, total_recv, device(at | {"z": z, "core": k})) for z in others for k in (0, 1)
        ]
        for hub_z, others in MEMBERS.items()
    }
    total_to_partner = remote(total, total, pair_send, total_recv, partner_dev)
    line_rest, plane_rest = line.at[pl.ds(0, LINE - 1)], plane.at[pl.ds(0, PLANE - 1)]

    @pl.when(is_hub)
    def _():
        pltpu.make_async_copy(line_rest, line_rest, line_recv).wait()
        plane_ref[...] = combine(line[...], count)
        for copy in to_peers:
            copy.start()

    def pass_on(kind, f):
        prev[kind, f].wait_recv()
        if kind:
            onward[kind, f].start()
        else:

            @pl.when(has_cross)
            def _():
                onward[kind, f].start()

    @pl.when(has_prev & jnp.logical_not(far))
    def _():
        pass_on(0, 0)
        pass_on(0, 1)

    for copy in vec_copies:
        copy.wait()

    @pl.when(is_hub)
    def _():
        pltpu.make_async_copy(plane_rest, plane_rest, plane_recv).wait()
        total[...] = combine(plane[...], count * LINE)
        total_to_partner.start()

    for hub_z, copies in to_members.items():

        @pl.when(is_hub & (at["z"] == hub_z))
        def _():
            for copy in copies:
                copy.start()

    @pl.when(jnp.logical_not(is_hub))
    def _():
        total_to_partner.wait_recv()

    @pl.when(has_prev & jnp.logical_not(far))
    def _():
        pass_on(1, 0)
        pass_on(1, 1)

    @pl.when(far)
    def _():
        pass_on(0, 0)

    mean, square = unpack(total[...])
    scale = lax.rsqrt(square / (count * LINE * PLANE) + 1e-06) * gain[...]
    half_scale, half_shift = 0.5 * scale, 0.5 * shift[...]

    def activate(f, y, src_f, src_y):
        h = (raw[src_f, src_y].astype(jnp.float32) - mean) * half_scale + half_shift
        act[f, y] = (h + h * jnp.tanh(h)).astype(jnp.bfloat16)

    top = jnp.where(r > 0, 0, 1)
    bottom = jnp.where(r < ROWS - 1, 3, 2)

    def window(a, frame_ids):
        parts = [act[frame_ids, b : b + 2] for b in range(3)]
        return jnp.concatenate([p.reshape(-1, channels) for p in parts], axis=-1)

    def tap(a, c):
        return jnp.concatenate([taps[a, b, c] for b in range(3)], axis=0)

    def dot(lhs, rhs):
        return jnp.dot(lhs, rhs, preferred_element_type=jnp.float32)

    for f in (2, 3):
        for y in (1, 2):
            activate(f, y, f, y)

    to_partner.wait_recv()

    @pl.when(has_cross)
    def _():
        to_cross.wait_recv()

    for f in (2, 3):
        activate(f, 0, f, top)
        activate(f, 3, f, bottom)
    taps_copy.wait()

    both, late = window(2, slice(2, 4)), window(1, slice(2, 3))
    for c in range(3):
        acc[c] = dot(both, tap(2, c)).reshape(acc.shape[1:])
        acc[c, 1] += dot(late, tap(1, c)).reshape(acc.shape[2:])

    @pl.when(far)
    def _():
        for kind, f in PIECES[1:]:
            pass_on(kind, f)

    src = [jnp.where(has_prev, f, 2) for f in range(2)]
    for f in range(2):
        for y in (1, 2):
            activate(f, y, src[f], y)

    def add(c, y, rows, b):
        for a in range(2):
            lhs = act[a:2, rows]
            acc[c, 0 : 2 - a, y] += dot(lhs.reshape(-1, channels), taps[a, b, c]).reshape(lhs.shape)

    for c in range(3):
        add(c, slice(0, 2), slice(1, 3), 1)
        add(c, 1, 1, 0)
        add(c, 0, 2, 2)

    @pl.when(has_prev & has_cross)
    def _():
        for f in range(2):
            onward[0, f].wait_recv()

    @pl.when(has_prev)
    def _():
        for f in range(2):
            onward[1, f].wait_recv()

    for f in range(2):
        activate(f, 0, src[f], top)
        activate(f, 3, src[f], bottom)
    for c in range(3):
        add(c, 0, 0, 0)
        add(c, 1, 3, 2)

    column = lax.broadcasted_iota(jnp.int32, (width, channels), 0)
    for f in range(2):
        for y in range(2):
            left, right = acc[0, f, y], acc[2, f, y]
            left = jnp.where(column == 0, left, pltpu.roll(left, 1, 0))
            right = jnp.where(column == width - 1, right, pltpu.roll(right, width - 1, 0))
            out[f, y] = (left + acc[1, f, y] + right + bias[...]).astype(jnp.bfloat16)

    @pl.when(has_next)
    def _():
        for copy in (prev[1, 0], prev[1, 1]):
            copy.wait_send()

    @pl.when(far_sender)
    def _():
        for f in range(2):
            prev[0, f].wait_send()

    @pl.when(has_cross)
    def _():
        to_cross.wait_send()

    to_partner.wait_send()

    @pl.when(has_prev & has_cross)
    def _():
        for f in range(2):
            onward[0, f].wait_send()

    @pl.when(has_prev)
    def _():
        for f in range(2):
            onward[1, f].wait_send()

    for piece, there in is_relay.items():

        @pl.when(there)
        def _():
            relay_out[piece].wait_send()

    for there, copy in to_hubs:

        @pl.when(there)
        def _():
            copy.wait_send()

    @pl.when(is_hub)
    def _():
        pltpu.make_async_copy(plane_rest, plane_rest, plane_send).wait()
        total_to_partner.wait_send()

    for hub_z, copies in to_members.items():

        @pl.when(is_hub & (at["z"] == hub_z))
        def _():
            sent = plane.at[pl.ds(0, len(copies))]
            pltpu.make_async_copy(sent, sent, total_send).wait()


def local(frames, norm_gain, norm_shift, conv_weight, conv_bias):
    frame_count, row_count, width, channels = frames.shape
    hbm = pl.BlockSpec(memory_space=pltpu.HBM)
    dma = pltpu.SemaphoreType.DMA
    return pl.pallas_call(
        kernel,
        out_shape=pltpu.VMEM(frames.shape, jnp.bfloat16),
        in_specs=[hbm] * 5,
        out_specs=pl.BlockSpec(memory_space=pltpu.VMEM),
        scratch_shapes=[
            pltpu.VMEM((4, 4, width, channels), jnp.bfloat16),
            pltpu.VMEM((4, 4, width, channels), jnp.bfloat16),
            pltpu.VMEM(conv_weight.shape, jnp.bfloat16),
            pltpu.VMEM((3, frame_count, row_count, width, channels), jnp.float32),
            pltpu.VMEM((width, channels), jnp.bfloat16),
            pltpu.VMEM((LINE, 1, channels // 2), jnp.float32),
            pltpu.VMEM((PLANE, 1, channels // 2), jnp.float32),
            pltpu.VMEM((1, channels // 2), jnp.float32),
            pltpu.VMEM((1, channels), jnp.float32),
            pltpu.VMEM((1, channels), jnp.float32),
            pltpu.VMEM((1, channels), jnp.float32),
            dma((3,)), dma, dma, dma((len(HUBS),)), dma, dma, dma, dma, dma, dma,
            dma((2, 2)), dma((2, 2)), dma((2,)), dma((2,)), dma((2, 2)), dma((2, 2)), dma, dma,
        ],
        compiler_params=pltpu.CompilerParams(
            collective_id=0, has_side_effects=True, vmem_limit_bytes=40 * 1024 * 1024
        ),
        name="norm_conv",
    )(
        *(
            pltpu.with_memory_space_constraint(x, pltpu.HBM)
            for x in (
                frames,
                norm_gain.reshape(1, channels),
                norm_shift.reshape(1, channels),
                conv_weight,
                conv_bias.reshape(1, channels),
            )
        )
    )


def solution(mesh):
    in_specs = (P("tm", "rows", None, None), P(), P(), P(), P())
    out_specs = P("tm", "rows", None, None)
    return jax.shard_map(local, mesh=mesh, in_specs=in_specs, out_specs=out_specs, check_vma=False)
```

```python
import jax
import jax.numpy as jnp
from jax import lax
from jax.experimental import pallas as pl
from jax.experimental.pallas import tpu as pltpu
from jax.sharding import PartitionSpec as P

GROUPS = 32
MESH = pl.DeviceIdType.MESH
TM, ROWS = 64, 8
SIZE = {"x": 4, "y": 8, "z": 8, "core": 2}
HUBS = (0, 1, 2)
MEMBERS = {0: (5, 6, 7), 2: (4, 3)}
LINE = SIZE["z"] * SIZE["core"]
PLANE = SIZE["x"] * SIZE["y"]
FAR = TM // 2
PIECES = ((0, 0), (0, 1), (1, 0), (1, 1))
RELAYS = {(0, 1): 7, (1, 0): 30, (1, 1): 23}


def coordinates(t, r):
    return {"x": (t >> 3) & 3, "y": ((t >> 5) << 2) + (r >> 1), "z": t & 7, "core": r & 1}


def device(at):
    y = at["y"]
    return {"tm": ((y >> 2) << 5) + (at["x"] << 3) + at["z"], "rows": ((y & 3) << 1) + at["core"]}


def plane_peers(at):
    nx, ny = SIZE["x"], SIZE["y"]
    steps = [(i, j) for i in range(nx) for j in range(ny)][1:]
    steps.sort(key=lambda step: min(step[0], nx - step[0]) + min(step[1], ny - step[1]), reverse=True)
    return [device(at | {"x": (at["x"] + i) & (nx - 1), "y": (at["y"] + j) & (ny - 1)}) for i, j in steps]


def signal(semaphore, where):
    pl.semaphore_signal(semaphore, inc=1, device_id=where, device_id_type=MESH)


def fold_channels(mean, square, n):
    lanes = mean.shape[-1]
    lane = lax.broadcasted_iota(jnp.int32, (2, lanes), 1)
    both = jnp.concatenate([mean, square], axis=0)
    for step in (1, 2, 4):
        ahead, behind = pltpu.roll(both, lanes - step, 1), pltpu.roll(both, step, 1)
        other = jnp.where((lane // step) % 2 == 0, ahead, behind)
        apart = both[0:1] - other[0:1]
        added = both + other
        both = jnp.concatenate([0.5 * added[0:1], added[1:2] + (0.5 * n * step) * apart * apart], axis=0)
    return both[0:1], both[1:2]


def pack(mean, square):
    half = mean.shape[-1] // 2
    lane = lax.broadcasted_iota(jnp.int32, (1, half), 1) % 4
    upper = jnp.where(lane == 1, mean[:, half:], square[:, half:])
    lower = jnp.where(lane == 0, mean[:, :half], square[:, :half])
    return jnp.where(lane % 2 == 0, lower, upper)


def unpack(packed):
    lane = lax.broadcasted_iota(jnp.int32, packed.shape, 1) % 4
    rows = jnp.concatenate([jnp.where(lane == k, packed, 0.0) for k in range(4)], axis=0)
    rows = group_fold(rows, 4)
    return jnp.concatenate([rows[0:1], rows[1:2]], axis=1), jnp.concatenate([rows[2:3], rows[3:4]], axis=1)


def combine(parts, n):
    added = jnp.sum(parts, axis=0)
    mean = added / parts.shape[0]
    apart = parts - mean[None]
    spread = pltpu.roll(jnp.sum(apart * apart, axis=0), 2, 1)
    lane = lax.broadcasted_iota(jnp.int32, mean.shape, 1) % 4
    return jnp.where(lane < 2, mean, added + n * spread)


def remote(src, dst, send, recv, where):
    return pltpu.make_async_remote_copy(
        src_ref=src, dst_ref=dst, send_sem=send, recv_sem=recv, device_id=where, device_id_type=MESH
    )


def group_fold(v, group_width):
    lanes = v.shape[-1]
    lane = lax.broadcasted_iota(jnp.int32, v.shape, v.ndim - 1)
    step = 1
    while step < group_width:
        ahead = pltpu.roll(v, lanes - step, v.ndim - 1)
        behind = pltpu.roll(v, step, v.ndim - 1)
        v = v + jnp.where((lane // step) % 2 == 0, ahead, behind)
        step *= 2
    return v


def kernel(
    frames, gain_hbm, shift_hbm, weight, bias_hbm, out,
    raw, act, taps, acc, relayed, line, plane, total, gain, shift, bias,
    vec_sem, own_sem, taps_sem, line_send, line_recv, plane_send, plane_recv, total_send, total_recv, pair_send, prev_send, prev_recv, row_send, row_recv,
    fwd_send, fwd_recv, relay_send, relay_recv,
):
    frame_count, row_count, width, channels = frames.shape
    group_width = channels // GROUPS
    cells = frame_count * row_count * width
    t, r = lax.axis_index("tm"), lax.axis_index("rows")
    has_prev, has_next = t > 0, t < TM - 1
    core = r & 1
    outer, inner = core, 1 - core
    has_cross = (r > 0) & (r < ROWS - 1)
    next_dev, prev_dev = {"tm": t + 1, "rows": r}, {"tm": t - 1, "rows": r}
    cross_dev, partner_dev = {"tm": t, "rows": r + 2 * core - 1}, {"tm": t, "rows": r + 1 - 2 * core}
    outer_slot, inner_slot = 3 - 3 * core, 3 * core

    at = coordinates(t, r)
    is_hub = (at["z"] <= HUBS[-1]) & (core == 1)
    hubs = [(at["z"] == z) & (core == 1) for z in HUBS]
    hub_devs = [device(at | {"z": z, "core": 1}) for z in HUBS]
    peers = plane_peers(at)
    line_slot, plane_slot = 2 * at["z"] + core, SIZE["y"] * at["x"] + at["y"]
    far_sender, far = t == FAR - 1, t == FAR
    is_relay = {piece: t == place for piece, place in RELAYS.items()}
    relay_devs = {piece: {"tm": place, "rows": r} for piece, place in RELAYS.items()}
    far_dev = {"tm": FAR, "rows": r}

    own_copy = pltpu.make_async_copy(frames, raw.at[2:4, 1:3], own_sem)

    barrier = pltpu.get_barrier_semaphore()

    for hub_z, others in MEMBERS.items():

        @pl.when((at["z"] >= min(others)) & (at["z"] <= max(others)))
        def _():
            signal(barrier, device(at | {"z": hub_z, "core": 1}))

    signal(barrier, partner_dev)
    greeted = [(has_prev, prev_dev), (has_cross, cross_dev)]
    greeted += [(far, where) for where in relay_devs.values()]
    greeted += [(there, {"tm": FAR - 1, "rows": r}) for there in is_relay.values()]
    for there, where in greeted:

        @pl.when(there)
        def _():
            signal(barrier, where)

    own_copy.start()

    @pl.when(is_hub)
    def _():
        for dz in (4, 3, 5, 2, 6, 1, 7, 0):
            for dk in range(0 if dz else 1, 2):
                signal(barrier, device(at | {"z": (at["z"] + dz) & 7, "core": (core + dk) & 1}))
        for where in peers:
            signal(barrier, where)

    vec_copies = [
        pltpu.make_async_copy(src, dst, vec_sem.at[i])
        for i, (src, dst) in enumerate(((gain_hbm, gain), (shift_hbm, shift), (bias_hbm, bias)))
    ]
    for copy in vec_copies:
        copy.start()
    own_copy.wait()
    taps_copy = pltpu.make_async_copy(weight, taps, taps_sem)
    taps_copy.start()

    mine = raw[2:4, 1:3].reshape(cells, channels).astype(jnp.float32)
    count = float(cells * group_width)
    channel_mean = jnp.sum(mine, axis=0, keepdims=True) * (1.0 / cells)
    centred = mine - channel_mean
    local_mean, local_square = fold_channels(channel_mean, jnp.sum(centred * centred, axis=0, keepdims=True), cells)

    greetings = 1 + jnp.where(is_hub, len(peers) - 1, 0) + len(hubs) + len(RELAYS) * far_sender.astype(jnp.int32)
    for hub_z, others in MEMBERS.items():
        greetings += jnp.where((at["z"] == hub_z) & (core == 1), 2 * len(others), 0)
    for there in [has_next, has_cross, *is_relay.values()]:
        greetings += there.astype(jnp.int32)
    pl.semaphore_wait(barrier, greetings)

    mine_ref = line.at[line_slot]
    mine_ref[...] = pack(local_mean, local_square)
    to_hubs = [
        (jnp.logical_not(here), remote(mine_ref, mine_ref, line_send.at[k], line_recv, where))
        for k, (here, where) in enumerate(zip(hubs, hub_devs))
    ]
    for there, copy in to_hubs:

        @pl.when(there)
        def _():
            copy.start()

    prev, onward, relay_in, relay_out = {}, {}, {}, {}
    for kind, f in PIECES:
        y, slot, where = ((outer, outer_slot, cross_dev), (inner, inner_slot, partner_dev))[kind]
        src, dst = frames.at[f, y], raw.at[f, 1 + y]
        prev[kind, f] = remote(src, dst, prev_send.at[kind, f], prev_recv.at[kind, f], next_dev)
        onward[kind, f] = remote(dst, raw.at[f, slot], fwd_send.at[kind, f], fwd_recv.at[kind, f], where)
        if (kind, f) in RELAYS:
            relay_in[kind, f] = remote(src, relayed, prev_send.at[kind, f], relay_recv, relay_devs[kind, f])
            relay_out[kind, f] = remote(relayed, dst, relay_send, prev_recv.at[kind, f], far_dev)
    to_cross = remote(frames.at[:, outer], raw.at[2:4, outer_slot], row_send.at[0], row_recv.at[0], cross_dev)
    to_partner = remote(frames.at[:, inner], raw.at[2:4, inner_slot], row_send.at[1], row_recv.at[1], partner_dev)

    @pl.when(has_next)
    def _():
        prev[0, 0].start()

    @pl.when(has_next & jnp.logical_not(far_sender))
    def _():
        prev[0, 1].start()

    @pl.when(far_sender)
    def _():
        for copy in relay_in.values():
            copy.start()

    @pl.when(has_cross)
    def _():
        to_cross.start()

    to_partner.start()

    for piece, there in is_relay.items():

        @pl.when(there)
        def _():
            relay_in[piece].wait_recv()
            relay_out[piece].start()

    plane_ref = plane.at[plane_slot]
    to_peers = [remote(plane_ref, plane_ref, plane_send, plane_recv, where) for where in peers]
    to_members = {
        hub_z: [
            remote(total, total, total_send, total_recv, device(at | {"z": z, "core": k})) for z in others for k in (0, 1)
        ]
        for hub_z, others in MEMBERS.items()
    }
    total_to_partner = remote(total, total, pair_send, total_recv, partner_dev)
    line_rest, plane_rest = line.at[pl.ds(0, LINE - 1)], plane.at[pl.ds(0, PLANE - 1)]

    @pl.when(is_hub)
    def _():
        pltpu.make_async_copy(line_rest, line_rest, line_recv).wait()
        plane_ref[...] = combine(line[...], count)
        for copy in to_peers:
            copy.start()

    @pl.when(has_next & jnp.logical_not(far_sender))
    def _():
        for f in range(2):
            prev[0, f].wait_send()
        for f in range(2):
            prev[1, f].start()

    def pass_on(kind, f):
        prev[kind, f].wait_recv()
        if kind:
            onward[kind, f].start()
        else:

            @pl.when(has_cross)
            def _():
                onward[kind, f].start()

    @pl.when(has_prev & jnp.logical_not(far))
    def _():
        pass_on(0, 0)
        pass_on(0, 1)

    for copy in vec_copies:
        copy.wait()

    @pl.when(is_hub)
    def _():
        pltpu.make_async_copy(plane_rest, plane_rest, plane_recv).wait()
        total[...] = combine(plane[...], count * LINE)
        total_to_partner.start()

    for hub_z, copies in to_members.items():

        @pl.when(is_hub & (at["z"] == hub_z))
        def _():
            for copy in copies:
                copy.start()

    @pl.when(jnp.logical_not(is_hub))
    def _():
        total_to_partner.wait_recv()

    @pl.when(has_prev & jnp.logical_not(far))
    def _():
        pass_on(1, 0)
        pass_on(1, 1)

    @pl.when(far)
    def _():
        pass_on(0, 0)

    mean, square = unpack(total[...])
    scale = lax.rsqrt(square / (count * LINE * PLANE) + 1e-06) * gain[...]
    half_scale, half_shift = 0.5 * scale, 0.5 * shift[...]

    def activate(f, y, src_f, src_y):
        h = (raw[src_f, src_y].astype(jnp.float32) - mean) * half_scale + half_shift
        act[f, y] = (h + h * jnp.tanh(h)).astype(jnp.bfloat16)

    top = jnp.where(r > 0, 0, 1)
    bottom = jnp.where(r < ROWS - 1, 3, 2)

    def window(a, frame_ids):
        parts = [act[frame_ids, b : b + 2] for b in range(3)]
        return jnp.concatenate([p.reshape(-1, channels) for p in parts], axis=-1)

    def tap(a, c):
        return jnp.concatenate([taps[a, b, c] for b in range(3)], axis=0)

    def dot(lhs, rhs):
        return jnp.dot(lhs, rhs, preferred_element_type=jnp.float32)

    for f in (2, 3):
        for y in (1, 2):
            activate(f, y, f, y)

    to_partner.wait_recv()

    @pl.when(has_cross)
    def _():
        to_cross.wait_recv()

    for f in (2, 3):
        activate(f, 0, f, top)
        activate(f, 3, f, bottom)
    taps_copy.wait()

    both, late = window(2, slice(2, 4)), window(1, slice(2, 3))
    for c in range(3):
        acc[c] = dot(both, tap(2, c)).reshape(acc.shape[1:])
        acc[c, 1] += dot(late, tap(1, c)).reshape(acc.shape[2:])

    @pl.when(far)
    def _():
        for kind, f in PIECES[1:]:
            pass_on(kind, f)

    src = [jnp.where(has_prev, f, 2) for f in range(2)]
    for f in range(2):
        for y in (1, 2):
            activate(f, y, src[f], y)

    def add(c, y, rows, b):
        for a in range(2):
            lhs = act[a:2, rows]
            acc[c, 0 : 2 - a, y] += dot(lhs.reshape(-1, channels), taps[a, b, c]).reshape(lhs.shape)

    for c in range(3):
        add(c, slice(0, 2), slice(1, 3), 1)
        add(c, 1, 1, 0)
        add(c, 0, 2, 2)

    @pl.when(has_prev & has_cross)
    def _():
        for f in range(2):
            onward[0, f].wait_recv()

    @pl.when(has_prev)
    def _():
        for f in range(2):
            onward[1, f].wait_recv()

    for f in range(2):
        activate(f, 0, src[f], top)
        activate(f, 3, src[f], bottom)
    for c in range(3):
        add(c, 0, 0, 0)
        add(c, 1, 3, 2)

    column = lax.broadcasted_iota(jnp.int32, (width, channels), 0)
    for f in range(2):
        for y in range(2):
            left, right = acc[0, f, y], acc[2, f, y]
            left = jnp.where(column == 0, left, pltpu.roll(left, 1, 0))
            right = jnp.where(column == width - 1, right, pltpu.roll(right, width - 1, 0))
            out[f, y] = (left + acc[1, f, y] + right + bias[...]).astype(jnp.bfloat16)

    @pl.when(has_next)
    def _():
        for copy in (prev[1, 0], prev[1, 1]):
            copy.wait_send()

    @pl.when(far_sender)
    def _():
        for f in range(2):
            prev[0, f].wait_send()

    @pl.when(has_cross)
    def _():
        to_cross.wait_send()

    to_partner.wait_send()

    @pl.when(has_prev & has_cross)
    def _():
        for f in range(2):
            onward[0, f].wait_send()

    @pl.when(has_prev)
    def _():
        for f in range(2):
            onward[1, f].wait_send()

    for piece, there in is_relay.items():

        @pl.when(there)
        def _():
            relay_out[piece].wait_send()

    for there, copy in to_hubs:

        @pl.when(there)
        def _():
            copy.wait_send()

    @pl.when(is_hub)
    def _():
        pltpu.make_async_copy(plane_rest, plane_rest, plane_send).wait()
        total_to_partner.wait_send()

    for hub_z, copies in to_members.items():

        @pl.when(is_hub & (at["z"] == hub_z))
        def _():
            sent = plane.at[pl.ds(0, len(copies))]
            pltpu.make_async_copy(sent, sent, total_send).wait()


def local(frames, norm_gain, norm_shift, conv_weight, conv_bias):
    frame_count, row_count, width, channels = frames.shape
    hbm = pl.BlockSpec(memory_space=pltpu.HBM)
    dma = pltpu.SemaphoreType.DMA
    return pl.pallas_call(
        kernel,
        out_shape=pltpu.VMEM(frames.shape, jnp.bfloat16),
        in_specs=[hbm] * 5,
        out_specs=pl.BlockSpec(memory_space=pltpu.VMEM),
        scratch_shapes=[
            pltpu.VMEM((4, 4, width, channels), jnp.bfloat16),
            pltpu.VMEM((4, 4, width, channels), jnp.bfloat16),
            pltpu.VMEM(conv_weight.shape, jnp.bfloat16),
            pltpu.VMEM((3, frame_count, row_count, width, channels), jnp.float32),
            pltpu.VMEM((width, channels), jnp.bfloat16),
            pltpu.VMEM((LINE, 1, channels // 2), jnp.float32),
            pltpu.VMEM((PLANE, 1, channels // 2), jnp.float32),
            pltpu.VMEM((1, channels // 2), jnp.float32),
            pltpu.VMEM((1, channels), jnp.float32),
            pltpu.VMEM((1, channels), jnp.float32),
            pltpu.VMEM((1, channels), jnp.float32),
            dma((3,)), dma, dma, dma((len(HUBS),)), dma, dma, dma, dma, dma, dma,
            dma((2, 2)), dma((2, 2)), dma((2,)), dma((2,)), dma((2, 2)), dma((2, 2)), dma, dma,
        ],
        compiler_params=pltpu.CompilerParams(
            collective_id=0, has_side_effects=True, vmem_limit_bytes=40 * 1024 * 1024
        ),
        name="norm_conv",
    )(
        *(
            pltpu.with_memory_space_constraint(x, pltpu.HBM)
            for x in (
                frames,
                norm_gain.reshape(1, channels),
                norm_shift.reshape(1, channels),
                conv_weight,
                conv_bias.reshape(1, channels),
            )
        )
    )


def solution(mesh):
    in_specs = (P("tm", "rows", None, None), P(), P(), P(), P())
    out_specs = P("tm", "rows", None, None)
    return jax.shard_map(local, mesh=mesh, in_specs=in_specs, out_specs=out_specs, check_vma=False)
```

```python
import jax
import jax.numpy as jnp
from jax import lax
from jax.experimental import pallas as pl
from jax.experimental.pallas import tpu as pltpu
from jax.sharding import PartitionSpec as P

GROUPS = 32
MESH = pl.DeviceIdType.MESH
TM, ROWS = 64, 8
SIZE = {"x": 4, "y": 8, "z": 8, "core": 2}
HUBS = (0, 1, 2)
MEMBERS = {0: (5, 6, 7), 2: (4, 3)}
LINE = SIZE["z"] * SIZE["core"]
PLANE = SIZE["x"] * SIZE["y"]
FAR = TM // 2
PIECES = ((0, 0), (0, 1), (1, 0), (1, 1))
RELAYS = {(0, 1): 7, (1, 0): 30, (1, 1): 23}


def coordinates(t, r):
    return {"x": (t >> 3) & 3, "y": ((t >> 5) << 2) + (r >> 1), "z": t & 7, "core": r & 1}


def device(at):
    y = at["y"]
    return {"tm": ((y >> 2) << 5) + (at["x"] << 3) + at["z"], "rows": ((y & 3) << 1) + at["core"]}


def plane_peers(at):
    nx, ny = SIZE["x"], SIZE["y"]
    steps = [(i, j) for i in range(nx) for j in range(ny)][1:]
    steps.sort(key=lambda step: min(step[0], nx - step[0]) + min(step[1], ny - step[1]), reverse=True)
    return [device(at | {"x": (at["x"] + i) & (nx - 1), "y": (at["y"] + j) & (ny - 1)}) for i, j in steps]


def signal(semaphore, where):
    pl.semaphore_signal(semaphore, inc=1, device_id=where, device_id_type=MESH)


def fold_channels(mean, square, n):
    lanes = mean.shape[-1]
    lane = lax.broadcasted_iota(jnp.int32, (2, lanes), 1)
    both = jnp.concatenate([mean, square], axis=0)
    for step in (1, 2, 4):
        ahead, behind = pltpu.roll(both, lanes - step, 1), pltpu.roll(both, step, 1)
        other = jnp.where((lane // step) % 2 == 0, ahead, behind)
        apart = both[0:1] - other[0:1]
        added = both + other
        both = jnp.concatenate([0.5 * added[0:1], added[1:2] + (0.5 * n * step) * apart * apart], axis=0)
    return both[0:1], both[1:2]


def pack(mean, square):
    half = mean.shape[-1] // 2
    lane = lax.broadcasted_iota(jnp.int32, (1, half), 1) % 4
    upper = jnp.where(lane == 1, mean[:, half:], square[:, half:])
    lower = jnp.where(lane == 0, mean[:, :half], square[:, :half])
    return jnp.where(lane % 2 == 0, lower, upper)


def unpack(packed):
    lane = lax.broadcasted_iota(jnp.int32, packed.shape, 1) % 4
    rows = jnp.concatenate([jnp.where(lane == k, packed, 0.0) for k in range(4)], axis=0)
    rows = group_fold(rows, 4)
    return jnp.concatenate([rows[0:1], rows[1:2]], axis=1), jnp.concatenate([rows[2:3], rows[3:4]], axis=1)


def combine(parts, n):
    added = jnp.sum(parts, axis=0)
    mean = added / parts.shape[0]
    apart = parts - mean[None]
    spread = pltpu.roll(jnp.sum(apart * apart, axis=0), 2, 1)
    lane = lax.broadcasted_iota(jnp.int32, mean.shape, 1) % 4
    return jnp.where(lane < 2, mean, added + n * spread)


def remote(src, dst, send, recv, where):
    return pltpu.make_async_remote_copy(
        src_ref=src, dst_ref=dst, send_sem=send, recv_sem=recv, device_id=where, device_id_type=MESH
    )


def group_fold(v, group_width):
    lanes = v.shape[-1]
    lane = lax.broadcasted_iota(jnp.int32, v.shape, v.ndim - 1)
    step = 1
    while step < group_width:
        ahead = pltpu.roll(v, lanes - step, v.ndim - 1)
        behind = pltpu.roll(v, step, v.ndim - 1)
        v = v + jnp.where((lane // step) % 2 == 0, ahead, behind)
        step *= 2
    return v


def kernel(
    frames, gain_hbm, shift_hbm, weight, bias_hbm, out,
    raw, act, taps, acc, relayed, line, plane, total, gain, shift, bias,
    vec_sem, own_sem, taps_sem, line_send, line_recv, plane_send, plane_recv, total_send, total_recv, pair_send, prev_send, prev_recv, row_send, row_recv,
    fwd_send, fwd_recv, relay_send, relay_recv,
):
    frame_count, row_count, width, channels = frames.shape
    group_width = channels // GROUPS
    cells = frame_count * row_count * width
    t, r = lax.axis_index("tm"), lax.axis_index("rows")
    has_prev, has_next = t > 0, t < TM - 1
    core = r & 1
    outer, inner = core, 1 - core
    has_cross = (r > 0) & (r < ROWS - 1)
    next_dev, prev_dev = {"tm": t + 1, "rows": r}, {"tm": t - 1, "rows": r}
    cross_dev, partner_dev = {"tm": t, "rows": r + 2 * core - 1}, {"tm": t, "rows": r + 1 - 2 * core}
    outer_slot, inner_slot = 3 - 3 * core, 3 * core

    at = coordinates(t, r)
    is_hub = (at["z"] <= HUBS[-1]) & (core == 1)
    hubs = [(at["z"] == z) & (core == 1) for z in HUBS]
    hub_devs = [device(at | {"z": z, "core": 1}) for z in HUBS]
    peers = plane_peers(at)
    line_slot, plane_slot = 2 * at["z"] + core, SIZE["y"] * at["x"] + at["y"]
    far_sender, far = t == FAR - 1, t == FAR
    is_relay = {piece: t == place for piece, place in RELAYS.items()}
    relay_devs = {piece: {"tm": place, "rows": r} for piece, place in RELAYS.items()}
    far_dev = {"tm": FAR, "rows": r}

    own_copy = pltpu.make_async_copy(frames, raw.at[2:4, 1:3], own_sem)

    barrier = pltpu.get_barrier_semaphore()

    for hub_z, others in MEMBERS.items():

        @pl.when((at["z"] >= min(others)) & (at["z"] <= max(others)))
        def _():
            signal(barrier, device(at | {"z": hub_z, "core": 1}))

    signal(barrier, partner_dev)
    greeted = [(has_prev, prev_dev), (has_cross, cross_dev)]
    greeted += [(far, where) for where in relay_devs.values()]
    greeted += [(there, {"tm": FAR - 1, "rows": r}) for there in is_relay.values()]
    for there, where in greeted:

        @pl.when(there)
        def _():
            signal(barrier, where)

    own_copy.start()

    @pl.when(is_hub)
    def _():
        for dz in (4, 3, 5, 2, 6, 1, 7, 0):
            for dk in range(0 if dz else 1, 2):
                signal(barrier, device(at | {"z": (at["z"] + dz) & 7, "core": (core + dk) & 1}))
        for where in peers:
            signal(barrier, where)

    vec_copies = [
        pltpu.make_async_copy(src, dst, vec_sem.at[i])
        for i, (src, dst) in enumerate(((gain_hbm, gain), (shift_hbm, shift), (bias_hbm, bias)))
    ]
    for copy in vec_copies:
        copy.start()
    own_copy.wait()
    taps_copy = pltpu.make_async_copy(weight, taps, taps_sem)
    taps_copy.start()

    mine = raw[2:4, 1:3].reshape(cells, channels).astype(jnp.float32)
    count = float(cells * group_width)
    channel_mean = jnp.sum(mine, axis=0, keepdims=True) * (1.0 / cells)
    centred = mine - channel_mean
    local_mean, local_square = fold_channels(channel_mean, jnp.sum(centred * centred, axis=0, keepdims=True), cells)

    greetings = 1 + jnp.where(is_hub, len(peers) - 1, 0) + len(hubs) + len(RELAYS) * far_sender.astype(jnp.int32)
    for hub_z, others in MEMBERS.items():
        greetings += jnp.where((at["z"] == hub_z) & (core == 1), 2 * len(others), 0)
    for there in [has_next, has_cross, *is_relay.values()]:
        greetings += there.astype(jnp.int32)
    pl.semaphore_wait(barrier, greetings)

    mine_ref = line.at[line_slot]
    mine_ref[...] = pack(local_mean, local_square)
    to_hubs = [
        (jnp.logical_not(here), remote(mine_ref, mine_ref, line_send.at[k], line_recv, where))
        for k, (here, where) in enumerate(zip(hubs, hub_devs))
    ]
    for there, copy in to_hubs:

        @pl.when(there)
        def _():
            copy.start()

    prev, onward, relay_in, relay_out = {}, {}, {}, {}
    for kind, f in PIECES:
        y, slot, where = ((outer, outer_slot, cross_dev), (inner, inner_slot, partner_dev))[kind]
        src, dst = frames.at[f, y], raw.at[f, 1 + y]
        prev[kind, f] = remote(src, dst, prev_send.at[kind, f], prev_recv.at[kind, f], next_dev)
        onward[kind, f] = remote(dst, raw.at[f, slot], fwd_send.at[kind, f], fwd_recv.at[kind, f], where)
        if (kind, f) in RELAYS:
            relay_in[kind, f] = remote(src, relayed, prev_send.at[kind, f], relay_recv, relay_devs[kind, f])
            relay_out[kind, f] = remote(relayed, dst, relay_send, prev_recv.at[kind, f], far_dev)
    to_cross = remote(frames.at[:, outer], raw.at[2:4, outer_slot], row_send.at[0], row_recv.at[0], cross_dev)
    to_partner = remote(frames.at[:, inner], raw.at[2:4, inner_slot], row_send.at[1], row_recv.at[1], partner_dev)

    @pl.when(has_next)
    def _():
        prev[0, 0].start()

    @pl.when(has_next & jnp.logical_not(far_sender))
    def _():
        prev[0, 1].start()

    @pl.when(far_sender)
    def _():
        for copy in relay_in.values():
            copy.start()

    @pl.when(has_cross)
    def _():
        to_cross.start()

    to_partner.start()

    for piece, there in is_relay.items():

        @pl.when(there)
        def _():
            relay_in[piece].wait_recv()
            relay_out[piece].start()

    plane_ref = plane.at[plane_slot]
    to_peers = [remote(plane_ref, plane_ref, plane_send, plane_recv, where) for where in peers]
    to_members = {
        hub_z: [
            remote(total, total, total_send, total_recv, device(at | {"z": z, "core": k})) for z in others for k in (0, 1)
        ]
        for hub_z, others in MEMBERS.items()
    }
    total_to_partner = remote(total, total, pair_send, total_recv, partner_dev)
    line_rest, plane_rest = line.at[pl.ds(0, LINE - 1)], plane.at[pl.ds(0, PLANE - 1)]

    @pl.when(is_hub)
    def _():
        pltpu.make_async_copy(line_rest, line_rest, line_recv).wait()
        plane_ref[...] = combine(line[...], count)
        for copy in to_peers:
            copy.start()

    @pl.when(has_next & jnp.logical_not(far_sender))
    def _():
        for f in range(2):
            prev[0, f].wait_send()
        for f in range(2):
            prev[1, f].start()

    def pass_on(kind, f):
        prev[kind, f].wait_recv()
        if kind:
            onward[kind, f].start()
        else:

            @pl.when(has_cross)
            def _():
                onward[kind, f].start()

    @pl.when(has_prev & jnp.logical_not(far))
    def _():
        pass_on(0, 0)
        pass_on(0, 1)

    to_partner.wait_recv()

    @pl.when(has_cross)
    def _():
        to_cross.wait_recv()

    taps_copy.wait()
    for copy in vec_copies:
        copy.wait()

    @pl.when(is_hub)
    def _():
        pltpu.make_async_copy(plane_rest, plane_rest, plane_recv).wait()
        total[...] = combine(plane[...], count * LINE)
        total_to_partner.start()

    for hub_z, copies in to_members.items():

        @pl.when(is_hub & (at["z"] == hub_z))
        def _():
            for copy in copies:
                copy.start()

    @pl.when(jnp.logical_not(is_hub))
    def _():
        total_to_partner.wait_recv()

    @pl.when(has_prev & jnp.logical_not(far))
    def _():
        pass_on(1, 0)
        pass_on(1, 1)

    @pl.when(far)
    def _():
        pass_on(0, 0)

    mean, square = unpack(total[...])
    scale = lax.rsqrt(square / (count * LINE * PLANE) + 1e-06) * gain[...]
    half_scale, half_shift = 0.5 * scale, 0.5 * shift[...]

    def activate(f, y, src_f, src_y):
        h = (raw[src_f, src_y].astype(jnp.float32) - mean) * half_scale + half_shift
        act[f, y] = (h + h * jnp.tanh(h)).astype(jnp.bfloat16)

    top = jnp.where(r > 0, 0, 1)
    bottom = jnp.where(r < ROWS - 1, 3, 2)

    def window(a, frame_ids):
        parts = [act[frame_ids, b : b + 2] for b in range(3)]
        return jnp.concatenate([p.reshape(-1, channels) for p in parts], axis=-1)

    def tap(a, c):
        return jnp.concatenate([taps[a, b, c] for b in range(3)], axis=0)

    def dot(lhs, rhs):
        return jnp.dot(lhs, rhs, preferred_element_type=jnp.float32)

    for f in (2, 3):
        for y in (1, 2):
            activate(f, y, f, y)

    for f in (2, 3):
        activate(f, 0, f, top)
        activate(f, 3, f, bottom)

    both, late = window(2, slice(2, 4)), window(1, slice(2, 3))
    for c in range(3):
        acc[c] = dot(both, tap(2, c)).reshape(acc.shape[1:])
        acc[c, 1] += dot(late, tap(1, c)).reshape(acc.shape[2:])

    @pl.when(far)
    def _():
        for kind, f in PIECES[1:]:
            pass_on(kind, f)

    src = [jnp.where(has_prev, f, 2) for f in range(2)]
    for f in range(2):
        for y in (1, 2):
            activate(f, y, src[f], y)

    def add(c, y, rows, b):
        for a in range(2):
            lhs = act[a:2, rows]
            acc[c, 0 : 2 - a, y] += dot(lhs.reshape(-1, channels), taps[a, b, c]).reshape(lhs.shape)

    for c in range(3):
        add(c, slice(0, 2), slice(1, 3), 1)
        add(c, 1, 1, 0)
        add(c, 0, 2, 2)

    @pl.when(has_prev & has_cross)
    def _():
        for f in range(2):
            onward[0, f].wait_recv()

    @pl.when(has_prev)
    def _():
        for f in range(2):
            onward[1, f].wait_recv()

    for f in range(2):
        activate(f, 0, src[f], top)
        activate(f, 3, src[f], bottom)
    for c in range(3):
        add(c, 0, 0, 0)
        add(c, 1, 3, 2)

    column = lax.broadcasted_iota(jnp.int32, (width, channels), 0)
    for f in range(2):
        for y in range(2):
            left, right = acc[0, f, y], acc[2, f, y]
            left = jnp.where(column == 0, left, pltpu.roll(left, 1, 0))
            right = jnp.where(column == width - 1, right, pltpu.roll(right, width - 1, 0))
            out[f, y] = (left + acc[1, f, y] + right + bias[...]).astype(jnp.bfloat16)

    @pl.when(has_next)
    def _():
        for copy in (prev[1, 0], prev[1, 1]):
            copy.wait_send()

    @pl.when(far_sender)
    def _():
        for f in range(2):
            prev[0, f].wait_send()

    @pl.when(has_cross)
    def _():
        to_cross.wait_send()

    to_partner.wait_send()

    @pl.when(has_prev & has_cross)
    def _():
        for f in range(2):
            onward[0, f].wait_send()

    @pl.when(has_prev)
    def _():
        for f in range(2):
            onward[1, f].wait_send()

    for piece, there in is_relay.items():

        @pl.when(there)
        def _():
            relay_out[piece].wait_send()

    for there, copy in to_hubs:

        @pl.when(there)
        def _():
            copy.wait_send()

    @pl.when(is_hub)
    def _():
        pltpu.make_async_copy(plane_rest, plane_rest, plane_send).wait()
        total_to_partner.wait_send()

    for hub_z, copies in to_members.items():

        @pl.when(is_hub & (at["z"] == hub_z))
        def _():
            sent = plane.at[pl.ds(0, len(copies))]
            pltpu.make_async_copy(sent, sent, total_send).wait()


def local(frames, norm_gain, norm_shift, conv_weight, conv_bias):
    frame_count, row_count, width, channels = frames.shape
    hbm = pl.BlockSpec(memory_space=pltpu.HBM)
    dma = pltpu.SemaphoreType.DMA
    return pl.pallas_call(
        kernel,
        out_shape=pltpu.VMEM(frames.shape, jnp.bfloat16),
        in_specs=[hbm] * 5,
        out_specs=pl.BlockSpec(memory_space=pltpu.VMEM),
        scratch_shapes=[
            pltpu.VMEM((4, 4, width, channels), jnp.bfloat16),
            pltpu.VMEM((4, 4, width, channels), jnp.bfloat16),
            pltpu.VMEM(conv_weight.shape, jnp.bfloat16),
            pltpu.VMEM((3, frame_count, row_count, width, channels), jnp.float32),
            pltpu.VMEM((width, channels), jnp.bfloat16),
            pltpu.VMEM((LINE, 1, channels // 2), jnp.float32),
            pltpu.VMEM((PLANE, 1, channels // 2), jnp.float32),
            pltpu.VMEM((1, channels // 2), jnp.float32),
            pltpu.VMEM((1, channels), jnp.float32),
            pltpu.VMEM((1, channels), jnp.float32),
            pltpu.VMEM((1, channels), jnp.float32),
            dma((3,)), dma, dma, dma((len(HUBS),)), dma, dma, dma, dma, dma, dma,
            dma((2, 2)), dma((2, 2)), dma((2,)), dma((2,)), dma((2, 2)), dma((2, 2)), dma, dma,
        ],
        compiler_params=pltpu.CompilerParams(
            collective_id=0, has_side_effects=True, vmem_limit_bytes=40 * 1024 * 1024
        ),
        name="norm_conv",
    )(
        *(
            pltpu.with_memory_space_constraint(x, pltpu.HBM)
            for x in (
                frames,
                norm_gain.reshape(1, channels),
                norm_shift.reshape(1, channels),
                conv_weight,
                conv_bias.reshape(1, channels),
            )
        )
    )


def solution(mesh):
    in_specs = (P("tm", "rows", None, None), P(), P(), P(), P())
    out_specs = P("tm", "rows", None, None)
    return jax.shard_map(local, mesh=mesh, in_specs=in_specs, out_specs=out_specs, check_vma=False)
```
